128 devices in a mesh: ckpt: 4 (over z_lo, core), wide: 32 (over z_hi, y, x).
Axes of the slice: x: 4, y: 4, z: 4 (z_hi: 2, z_lo: 2; z = z_hi * 2 + z_lo), core: 2. Of those that a mesh axis runs over, the one named last changes fastest.
Arguments:
- codes: bfloat16 [4, 32, 8192, 1024], P('ckpt', 'wide'), may hold values from -4 to 4
- scales: float32 [4, 32, 8192, 8], P('ckpt', 'wide'), may hold values from 0.5 to 5
- example_ids: int32 [32, 8192], P('wide'), may hold values from 0 to 8191, each once within a row
- targets: bfloat16 [4096, 4096], P('wide'), may hold values from -0.09375 to 0.09375
- owners: int32 [6], replicated, may hold values from 0 to 31, as said below
Outputs:
- scores: float32 [32, 8192, 768], P('wide', 'ckpt')
The draws below stay inside these ranges and needn't reach their ends.
Inputs may be any that keep to these rules, and one draw needn't show every extreme that they name: `example_ids`: each row is a permutation of the 8192 examples of its group. Distinct owners; owner 0 and owner 32 - 1 are always among them.
All inputs are finite; a program needn't handle non-finite values.
Results may differ from the reference program's by a relative error of at most 0.0029.
Values may be sent and summed in bfloat16 or wider, within the bound.
No kernel may reach another device: no remote copies, remote signals or barrier semaphores. Data moves between devices by JAX's collectives and lax.ppermute only.
A program may use at most 192 MiB of HBM per device.

```python
import math
import jax
import jax.numpy as jnp
from jax import lax

K = 1024
C = 4
QB = 128
TBLK = 128
ROUNDS = 6
GROUPS = 32
GROUP_ROWS = 8192
TARGETS = 768
OWNED = 4096
CK = 4096
QBLOCKS = 8


def draw_owners(key, part):
    first_key = jax.random.fold_in(key, 17)
    second_key = jax.random.fold_in(key, 29)
    middle = 1 + jax.random.permutation(first_key, GROUPS - 2).astype(jnp.int32)
    picked = jnp.concatenate([middle[:ROUNDS - 2], jnp.array([0, GROUPS - 1], jnp.int32)])
    return jax.random.permutation(second_key, picked).astype(jnp.int32)


def shard_levels(stream_key, extent, pieces, low, high):
    factor_of = 1.0
    for dim, shards_of in pieces:
        draws = jax.random.uniform(jax.random.fold_in(jax.random.fold_in(stream_key, 6), dim), (shards_of,), jnp.float32, low / len(pieces), high / len(pieces))
        factor_of = factor_of * jnp.repeat(jnp.exp(draws), extent[dim] // shards_of).reshape((-1,) + (1,) * (len(extent) - 1 - dim))
    return factor_of


def noise(key, extent, spread, most, cuts=(), kind=jnp.bfloat16):
    factor_of = shard_levels(key, extent, cuts, -0.22, 0.18) if cuts else 1.0
    entries = jax.random.normal(key, extent, jnp.float32) * spread * factor_of
    return jnp.minimum(jnp.maximum(entries, -most), most).astype(kind)


def setup_inputs(seed: int = 0) -> dict:
    splits = jax.random.split(jax.random.key(seed), 6)
    return {
        "codes": noise(splits[0], (C, GROUPS, GROUP_ROWS, K), 1.0, 4.0, ((0, 4), (1, 32))),
        "scales": jnp.clip(jnp.exp(math.log(5.0) - 2.3025851 * jax.random.uniform(splits[1], (C, GROUPS, GROUP_ROWS, QBLOCKS), jnp.float32) ** shard_levels(splits[1], (C, GROUPS, GROUP_ROWS, QBLOCKS), ((0, 4), (1, 32)), -0.2, 0.2)), 0.5, 5.0),
        "example_ids": jax.vmap(lambda own: jax.random.permutation(own, GROUP_ROWS))(jax.random.split(splits[2], GROUPS)).reshape((GROUPS, GROUP_ROWS)).astype(jnp.int32),
        "targets": noise(splits[3], (OWNED, CK), CK ** -0.5, 0.09375, ((0, 32),)),
        "owners": draw_owners(jax.random.fold_in(splits[5], 71), 0),
    }


def reference(codes, scales, example_ids, targets, owners):
    blocks = targets.reshape(GROUPS, TBLK, CK)
    chosen = jnp.take(blocks, owners, axis=0).reshape(TARGETS, CK)

    def one_group(group):
        group_codes = lax.dynamic_index_in_dim(codes, group, 1, keepdims=False)
        group_scales = lax.dynamic_index_in_dim(scales, group, 1, keepdims=False)
        feats = (group_codes.astype(jnp.float32) * jnp.repeat(group_scales, QB, axis=-1)).astype(jnp.bfloat16)
        ids = lax.dynamic_index_in_dim(example_ids, group, 0, keepdims=False)
        picked = jnp.take(feats, ids, axis=1)
        resident = jnp.transpose(picked, (1, 0, 2)).reshape(GROUP_ROWS, CK)
        total = lax.dot_general(resident, chosen, (((1,), (1,)), ((), ())), preferred_element_type=jnp.float32)
        return total * (1.0 / C)

    return lax.map(one_group, jnp.arange(GROUPS, dtype=jnp.int32))
```

```python
import functools

import jax
import jax.numpy as jnp
from jax import lax
from jax.experimental import pallas as pl
from jax.experimental.pallas import tpu as pltpu
from jax.sharding import PartitionSpec as P

BF = jnp.bfloat16
F32 = jnp.float32
LANES = 128
PIECES = 8
TB = 128
RB = 512
VMEM = pl.BlockSpec(memory_space=pltpu.VMEM)
ANY = pl.BlockSpec(memory_space=pl.ANY)
NT = (((1,), (1,)), ((), ()))


def gather_body(parts, q_ref, ids_ref, codes_ref, sc_ref, *rest):
    outs = rest[: len(parts)]
    wide, held, stage, sem_in, sem_out = rest[len(parts) :]
    rows, width = held.shape
    nb = width // LANES
    piece = rows // PIECES
    quarter = rows // 4

    def load(i):
        at = pl.ds(i * piece, piece)
        return pltpu.make_async_copy(codes_ref.at[at], held.at[at], sem_in.at[i])

    for i in range(PIECES):
        load(i).start()
    spread = (
        lax.broadcasted_iota(jnp.int32, (3 * nb, width), 0) % nb
        == lax.broadcasted_iota(jnp.int32, (3 * nb, width), 1) // LANES
    ).astype(F32).astype(BF)
    for i in range(PIECES):
        load(i).wait()
        r0 = i * piece
        s = sc_ref[:, r0 : r0 + piece]
        hi = s.astype(BF)
        left = s - hi.astype(F32)
        mid = left.astype(BF)
        low = (left - mid.astype(F32)).astype(BF)
        three = jnp.concatenate([hi, mid, low], axis=0)
        scale = lax.dot_general(three, spread, (((0,), (0,)), ((), ())), preferred_element_type=F32)
        for b in range(nb):
            cols = slice(b * LANES, (b + 1) * LANES)
            wide[pl.ds(r0 * nb + b, piece, stride=nb), :] = (
                held[r0 : r0 + piece, cols].astype(F32) * scale[:, cols]
            )
    q = q_ref[0]
    for p, x in enumerate(parts):
        src = (q ^ x) * quarter

        def block(t, carry, p=p, src=src):
            o = pl.multiple_of(t * TB, TB)
            for r in range(TB):
                e = ids_ref[src + o + r]
                stage[r * nb : (r + 1) * nb, :] = wide[pl.ds(pl.multiple_of(e * nb, nb), nb), :]
            d = pl.multiple_of(p * quarter + o, TB)
            for b in range(nb):
                held[pl.ds(d, TB), b * LANES : (b + 1) * LANES] = stage[
                    pl.ds(b, TB, stride=nb), :
                ].astype(BF)
            pltpu.make_async_copy(
                held.at[pl.ds(d, TB)], outs[p].at[pl.ds(o, TB)], sem_out.at[p]
            ).start()
            return carry

        lax.fori_loop(0, quarter // TB, block, 0)
    for p in range(len(parts)):
        pltpu.make_async_copy(
            held.at[pl.ds(p * quarter, quarter)], outs[p], sem_out.at[p]
        ).wait()


def gather(parts, q, ids, codes, scales_t):
    rows, width = codes.shape
    nb = scales_t.shape[0]
    return pl.pallas_call(
        functools.partial(gather_body, parts),
        grid_spec=pltpu.PrefetchScalarGridSpec(
            num_scalar_prefetch=2,
            grid=(),
            in_specs=[ANY, VMEM],
            out_specs=[ANY] * len(parts),
            scratch_shapes=[
                pltpu.VMEM((rows * nb, LANES), F32),
                pltpu.VMEM((rows, width), BF),
                pltpu.VMEM((TB * nb, LANES), F32),
                pltpu.SemaphoreType.DMA((PIECES,)),
                pltpu.SemaphoreType.DMA((len(parts),)),
            ],
        ),
        out_shape=[jax.ShapeDtypeStruct((rows // 4, width), BF)] * len(parts),
        compiler_params=pltpu.CompilerParams(vmem_limit_bytes=58 * 1024 * 1024),
        cost_estimate=pl.CostEstimate(flops=40_000_000_000, bytes_accessed=50_000_000, transcendentals=0),
        name="gather_features",
    )(q, ids, codes, scales_t)


def pick_body(owners_ref, rec_ref, out_ref):
    n, rounds = out_ref.shape[:2]
    for r in range(rounds):
        piece = rec_ref[owners_ref[r]]
        for d in range(n):
            out_ref[d, r] = piece


def pick(owners, rec):
    n, h, w = rec.shape
    rounds = owners.shape[0]
    return pl.pallas_call(
        pick_body,
        grid_spec=pltpu.PrefetchScalarGridSpec(
            num_scalar_prefetch=1, grid=(), in_specs=[VMEM], out_specs=VMEM
        ),
        out_shape=jax.ShapeDtypeStruct((n, rounds, h, w), BF),
        name="pick_pieces",
    )(owners, rec)


def assemble(raw_ref, t_ref):
    n, rounds, h, w = raw_ref.shape
    cuts = t_ref.shape[1] // w
    for r in range(rounds):
        for g in range(n // cuts):
            for c in range(cuts):
                row = r * (n // cuts) * h + g * h
                t_ref[row : row + h, c * w : (c + 1) * w] = raw_ref[g * cuts + c, r]


def send_body(mine_ref, other_ref, tm_ref, to_ref, out_ref, tm, to):
    @pl.when(pl.program_id(0) == 0)
    def _():
        assemble(tm_ref, tm)
        assemble(to_ref, to)

    acc = lax.dot_general(mine_ref[...], tm[...], NT, preferred_element_type=F32)
    acc += lax.dot_general(other_ref[...], to[...], NT, preferred_element_type=F32)
    out_ref[...] = acc.astype(BF)


def final_body(scale, mine_ref, other_ref, tm_ref, to_ref, got_ref, prev_ref, out_ref, tm, to):
    @pl.when(pl.program_id(0) == 0)
    def _():
        assemble(tm_ref, tm)
        assemble(to_ref, to)

    acc = lax.dot_general(mine_ref[...], tm[...], NT, preferred_element_type=F32)
    acc += lax.dot_general(other_ref[...], to[...], NT, preferred_element_type=F32)
    out_ref[...] = (acc + got_ref[...].astype(F32)) * scale


def common_specs(mine, raw, first, count):
    rows, width = mine.shape
    n, _, h, w = raw.shape
    feats = pl.BlockSpec((RB, width), lambda i: (i, 0))
    targets = pl.BlockSpec((n, count, h, w), lambda i: (0, first // count, 0, 0))
    per_round = n * h * w // width
    scratch = [pltpu.VMEM((count * per_round, width), BF)] * 2
    return rows, count * per_round, [feats, feats, targets, targets], scratch


def send_scores(mine, other, raw_m, raw_o, first, count):
    rows, cols, specs, scratch = common_specs(mine, raw_m, first, count)
    return pl.pallas_call(
        send_body,
        grid=(rows // RB,),
        in_specs=specs,
        out_specs=pl.BlockSpec((RB, cols), lambda i: (i, 0)),
        scratch_shapes=scratch,
        out_shape=jax.ShapeDtypeStruct((rows, cols), BF),
        compiler_params=pltpu.CompilerParams(vmem_limit_bytes=32 * 1024 * 1024),
        name="send_scores",
    )(mine, other, raw_m, raw_o)


def final_scores(scale, mine, other, raw_m, raw_o, got, prev, first, count, total):
    rows, cols, specs, scratch = common_specs(mine, raw_m, first, count)
    if prev is None:
        prev, alias = jnp.zeros((8, LANES), F32), {}
    else:
        alias = {5: 0}
    return pl.pallas_call(
        functools.partial(final_body, scale),
        grid=(rows // RB,),
        in_specs=specs + [pl.BlockSpec((RB, cols), lambda i: (i, 0)), ANY],
        out_specs=pl.BlockSpec((RB, cols), lambda i: (i, first // count)),
        scratch_shapes=scratch,
        out_shape=jax.ShapeDtypeStruct((rows, total), F32),
        input_output_aliases=alias,
        compiler_params=pltpu.CompilerParams(vmem_limit_bytes=32 * 1024 * 1024),
        name="final_scores",
    )(mine, other, raw_m, raw_o, got, prev)


def per_device(codes, scales, example_ids, targets, owners):
    n_ckpt = lax.axis_size("ckpt")
    n_wide = lax.axis_size("wide")
    q = lax.axis_index("ckpt")
    width = codes.shape[-1]
    codes, scales_t, ids = codes[0, 0], scales[0, 0].T, example_ids[0]
    other_core = [(i, i ^ 1) for i in range(n_ckpt)]
    other_chip = [(i, i ^ 2) for i in range(n_ckpt)]

    cuts = 4
    rows = targets.shape[0]
    h, w = rows * cuts // n_wide, width // cuts
    own = lax.dynamic_slice_in_dim(targets, q * width, width, 1)
    pieces = own.reshape(n_wide // cuts, h, cuts, w).transpose(0, 2, 1, 3).reshape(n_wide, h, w)
    rec = lax.all_to_all(pieces, "wide", 0, 0, tiled=True)
    raw_m = lax.all_to_all(pick(owners, rec), "wide", 0, 0, tiled=True)
    raw_o = lax.ppermute(raw_m, "ckpt", other_core)

    q1 = q.reshape(1)
    to_partner_far, mine_far = gather((3, 2), q1, ids, codes, scales_t)
    other_far = lax.ppermute(to_partner_far, "ckpt", other_core)
    to_partner_near, mine_near = gather((1, 0), q1, ids, codes, scales_t)
    other_near = lax.ppermute(to_partner_near, "ckpt", other_core)

    rounds = owners.shape[0]
    count = 2
    got = []
    for first in range(0, rounds, count):
        part = send_scores(mine_far, other_far, raw_m, raw_o, first, count)
        got.append(lax.ppermute(part, "ckpt", other_chip))
    out = None
    for k, first in enumerate(range(0, rounds, count)):
        out = final_scores(
            1.0 / n_ckpt, mine_near, other_near, raw_m, raw_o, got[k], out, first, count, rounds * rows
        )
    return out[None]


def solution(mesh):
    return jax.shard_map(
        per_device,
        mesh=mesh,
        in_specs=(
            P("ckpt", "wide", None, None),
            P("ckpt", "wide", None, None),
            P("wide", None),
            P("wide", None),
            P(),
        ),
        out_specs=P("wide", "ckpt", None),
        check_vma=False,
    )
```

```python
import functools

import jax
import jax.numpy as jnp
from jax import lax
from jax.experimental import pallas as pl
from jax.experimental.pallas import tpu as pltpu
from jax.sharding import PartitionSpec as P

BF = jnp.bfloat16
F32 = jnp.float32
I32 = jnp.int32
LANES = 128
PIECES = 8
TB = 128
CUTS = 4
MIB = 1024 * 1024
VMEM = pl.BlockSpec(memory_space=pltpu.VMEM)
SMEM = pl.BlockSpec(memory_space=pltpu.SMEM)
ANY = pl.BlockSpec(memory_space=pl.ANY)
NT = (((1,), (1,)), ((), ()))
TOKEN = jax.ShapeDtypeStruct((1,), I32)


def params(mib):
    return pltpu.CompilerParams(vmem_limit_bytes=mib * MIB)


def grid_of(scalars, grid, ins, outs, scratch=()):
    return pltpu.PrefetchScalarGridSpec(
        num_scalar_prefetch=scalars, grid=grid, in_specs=ins, out_specs=outs, scratch_shapes=scratch
    )


def gather_body(parts, q_ref, ids_ref, codes_ref, sc_ref, *rest):
    n = len(parts)
    outs, token = rest[:n], rest[n]
    wide, held, stage, sem_in, sem_out = rest[n + 1 :]
    rows, width = held.shape
    nb = width // LANES
    piece = rows // PIECES
    quarter = rows // 4

    def load(i):
        at = pl.ds(i * piece, piece)
        return pltpu.make_async_copy(codes_ref.at[at], held.at[at], sem_in.at[i])

    for i in range(PIECES):
        load(i).start()
    spread = (
        lax.broadcasted_iota(I32, (3 * nb, width), 0) % nb
        == lax.broadcasted_iota(I32, (3 * nb, width), 1) // LANES
    ).astype(F32).astype(BF)
    for i in range(PIECES):
        load(i).wait()
        r0 = i * piece
        s = sc_ref[:, r0 : r0 + piece]
        hi = s.astype(BF)
        left = s - hi.astype(F32)
        mid = left.astype(BF)
        low = (left - mid.astype(F32)).astype(BF)
        three = jnp.concatenate([hi, mid, low], axis=0)
        scale = lax.dot_general(three, spread, (((0,), (0,)), ((), ())), preferred_element_type=F32)
        for b in range(nb):
            cols = slice(b * LANES, (b + 1) * LANES)
            wide[pl.ds(r0 * nb + b, piece, stride=nb), :] = (
                held[r0 : r0 + piece, cols].astype(F32) * scale[:, cols]
            )
    q = q_ref[0]
    token[0] = q
    for p, x in enumerate(parts):
        src = (q ^ x) * quarter

        def block(t, carry, p=p, src=src):
            o = pl.multiple_of(t * TB, TB)
            for r in range(TB):
                e = ids_ref[src + o + r]
                stage[r * nb : (r + 1) * nb, :] = wide[pl.ds(pl.multiple_of(e * nb, nb), nb), :]
            d = pl.multiple_of(p * quarter + o, TB)
            for b in range(nb):
                held[pl.ds(d, TB), b * LANES : (b + 1) * LANES] = stage[
                    pl.ds(b, TB, stride=nb), :
                ].astype(BF)
            pltpu.make_async_copy(
                held.at[pl.ds(d, TB)], outs[p].at[pl.ds(o, TB)], sem_out.at[p]
            ).start()
            return carry

        lax.fori_loop(0, quarter // TB, block, 0)
    for p in range(n):
        pltpu.make_async_copy(
            held.at[pl.ds(p * quarter, quarter)], outs[p], sem_out.at[p]
        ).wait()


def gather(parts, q, ids, codes, scales_t):
    rows, width = codes.shape
    nb = scales_t.shape[0]
    n = len(parts)
    return pl.pallas_call(
        functools.partial(gather_body, parts),
        grid_spec=grid_of(
            2,
            (),
            [ANY, VMEM],
            [ANY] * n + [SMEM],
            [
                pltpu.VMEM((rows * nb, LANES), F32),
                pltpu.VMEM((rows, width), BF),
                pltpu.VMEM((TB * nb, LANES), F32),
                pltpu.SemaphoreType.DMA((PIECES,)),
                pltpu.SemaphoreType.DMA((n,)),
            ],
        ),
        out_shape=[jax.ShapeDtypeStruct((rows // 4, width), BF)] * n + [TOKEN],
        compiler_params=params(54),
        name="gather_features",
    )(q, ids, codes, scales_t)


def pick_body(owners_ref, q_ref, rec_ref, held_ref, out_ref, token, held_out):
    token[0] = q_ref[0]
    n, rounds = out_ref.shape[:2]
    for r in range(rounds):
        piece = rec_ref[owners_ref[r]]
        for d in range(n):
            out_ref[d, r] = piece


def pick(owners, q, rec, held):
    n, h, w = rec.shape
    return pl.pallas_call(
        pick_body,
        grid_spec=grid_of(2, (), [VMEM, ANY], [VMEM, SMEM, ANY]),
        out_shape=[
            jax.ShapeDtypeStruct((n, owners.shape[0], h, w), BF),
            TOKEN,
            jax.ShapeDtypeStruct(held.shape, held.dtype),
        ],
        input_output_aliases={3: 2},
        compiler_params=params(8),
        name="pick_pieces",
    )(owners, q, rec, held)


def tie_body(q_ref, x_ref, y_ref, x_out, y_out, token):
    token[0] = q_ref[0]


def tie(q, x, y):
    return pl.pallas_call(
        tie_body,
        grid_spec=grid_of(1, (), [ANY, ANY], [ANY, ANY, SMEM]),
        out_shape=[jax.ShapeDtypeStruct(a.shape, a.dtype) for a in (x, y)] + [TOKEN],
        input_output_aliases={1: 0, 2: 1},
        compiler_params=params(56),
        name="tie",
    )(q, x, y)


def lay(raw_ref, t_ref):
    n, rounds, h, w = raw_ref.shape
    per = t_ref.shape[0] // rounds
    for r in range(rounds):
        for d in range(n):
            row = r * per + d // CUTS * h
            t_ref[row : row + h, d % CUTS * w : (d % CUTS + 1) * w] = raw_ref[d, r]


def dots(mine_ref, other_ref, tm, to):
    acc = lax.dot_general(mine_ref[...], tm[...], NT, preferred_element_type=F32)
    return acc + lax.dot_general(other_ref[...], to[...], NT, preferred_element_type=F32)


def send_body(q_ref, mine_ref, other_ref, tm_ref, to_ref, *rest):
    out_ref, token, tm, to = rest[-4:]
    token[0] = q_ref[0]

    @pl.when(pl.program_id(0) == 0)
    def _():
        lay(tm_ref, tm)
        lay(to_ref, to)

    out_ref[...] = dots(mine_ref, other_ref, tm, to).astype(BF)


def send_scores(q, mine, other, raw_m, raw_o, pair, per, start, count, after=(), block=512):
    width = mine.shape[1]
    n, _, h, w = raw_m.shape
    feats = pl.BlockSpec((block, width), lambda i, *_: (i + start // block, 0))
    targets = pl.BlockSpec((n, 2, h, w), lambda i, *_: (0, pair, 0, 0))
    return pl.pallas_call(
        send_body,
        grid_spec=grid_of(
            1,
            (count // block,),
            [feats, feats, targets, targets] + [ANY] * len(after),
            [pl.BlockSpec((block, 2 * per), lambda i, *_: (i, 0)), SMEM],
            [pltpu.VMEM((2 * per, width), BF)] * 2,
        ),
        out_shape=[jax.ShapeDtypeStruct((count, 2 * per), BF), TOKEN],
        compiler_params=params(16),
        name="send_scores",
    )(q, mine, other, raw_m, raw_o, *after)


def near_body(scale, q_ref, mine_ref, other_ref, tm_ref, to_ref, out_ref, tm, to):
    @pl.when(pl.program_id(0) == 0)
    def _():
        lay(tm_ref, tm)
        lay(to_ref, to)

    out_ref[...] = dots(mine_ref, other_ref, tm, to) * scale


def near_scores(q, scale, mine, other, raw_m, raw_o, per, block=256):
    rows, width = mine.shape
    total = per * raw_m.shape[1]
    feats = pl.BlockSpec((block, width), lambda i, *_: (i, 0))
    raw = pl.BlockSpec(raw_m.shape, lambda i, *_: (0, 0, 0, 0))
    return pl.pallas_call(
        functools.partial(near_body, scale),
        grid_spec=grid_of(
            1,
            (rows // block,),
            [feats, feats, raw, raw],
            pl.BlockSpec((block, total), lambda i, *_: (i, 0)),
            [pltpu.VMEM((total, width), BF)] * 2,
        ),
        out_shape=jax.ShapeDtypeStruct((rows, total), F32),
        compiler_params=params(32),
        name="near_scores",
    )(q, mine, other, raw_m, raw_o)


def add_body(scale, got_ref, old_ref, out_ref):
    out_ref[...] = old_ref[...] + got_ref[...].astype(F32) * scale


def add_scores(scale, got, out, pair, start, block=512):
    count, cols = got.shape
    cell = pl.BlockSpec((block, cols), lambda i: (i + start // block, pair))
    return pl.pallas_call(
        functools.partial(add_body, scale),
        grid=(count // block,),
        in_specs=[pl.BlockSpec((block, cols), lambda i: (i, 0)), cell],
        out_specs=cell,
        out_shape=jax.ShapeDtypeStruct(out.shape, F32),
        input_output_aliases={1: 0},
        compiler_params=params(16),
        name="add_scores",
    )(got, out)


def per_device(codes, scales, example_ids, targets, owners):
    n_ckpt = lax.axis_size("ckpt")
    n_wide = lax.axis_size("wide")
    q = lax.axis_index("ckpt")
    width = codes.shape[-1]
    codes, scales_t, ids = codes[0, 0], scales[0, 0].T, example_ids[0]
    other_core = [(i, i ^ 1) for i in range(n_ckpt)]
    other_chip = [(i, i ^ 2) for i in range(n_ckpt)]
    per = targets.shape[0]
    quarter = ids.shape[0] // n_ckpt
    scale = 1.0 / n_ckpt
    q1 = q.reshape(1)

    h, w = per * CUTS // n_wide, width // CUTS
    own = lax.dynamic_slice_in_dim(targets, q * width, width, 1)
    pieces = own.reshape(n_wide // CUTS, h, CUTS, w).transpose(0, 2, 1, 3).reshape(n_wide, h, w)
    rec = lax.all_to_all(pieces, "wide", 0, 0, tiled=True)
    to_far, tok = gather((3,), q1, ids, codes, scales_t)

    picked, tok, to_far = pick(owners, tok, rec, to_far)
    other_far = lax.ppermute(to_far, "ckpt", other_core)
    raw_m = lax.all_to_all(picked, "wide", 0, 0, tiled=True)
    mine_far, to_near, mine_near, tok = gather((2, 1, 0), tok, ids, codes, scales_t)
    raw_m, to_near, tok = tie(tok, raw_m, to_near)
    raw_o = lax.ppermute(raw_m, "ckpt", other_core)

    other_near = lax.ppermute(to_near, "ckpt", other_core)

    sent = []
    for pair, start, count in plan(owners.shape[0] // 2, quarter):
        after = [sent[-3][0]] if len(sent) > 2 else []
        part, tok = send_scores(
            tok, mine_far, other_far, raw_m, raw_o, pair, per, start, count, after
        )
        sent.append((lax.ppermute(part, "ckpt", other_chip), pair, start))

    out = near_scores(tok, scale, mine_near, other_near, raw_m, raw_o, per)
    for got, pair, start in sent:
        out = add_scores(scale, got, out, pair, start)
    return out[None]


def plan(pairs, rows):
    for pair in range(pairs):
        cuts = 2 if pair in (0, pairs - 1) else 1
        for c in range(cuts):
            yield pair, c * (rows // cuts), rows // cuts


def solution(mesh):
    return jax.shard_map(
        per_device,
        mesh=mesh,
        in_specs=(
            P("ckpt", "wide", None, None),
            P("ckpt", "wide", None, None),
            P("wide", None),
            P("wide", None),
            P(),
        ),
        out_specs=P("wide", "ckpt", None),
        check_vma=False,
    )
```

```python
import functools

import jax
import jax.numpy as jnp
from jax import lax
from jax.experimental import pallas as pl
from jax.experimental.pallas import tpu as pltpu
from jax.sharding import PartitionSpec as P

BF = jnp.bfloat16
F32 = jnp.float32
I32 = jnp.int32
LANES = 128
PIECES = 8
TB = 128
CUTS = 4
AHEAD = 4
MIB = 1024 * 1024
VMEM = pl.BlockSpec(memory_space=pltpu.VMEM)
SMEM = pl.BlockSpec(memory_space=pltpu.SMEM)
ANY = pl.BlockSpec(memory_space=pl.ANY)
NT = (((1,), (1,)), ((), ()))
TOKEN = jax.ShapeDtypeStruct((1,), I32)


def params(mib):
    return pltpu.CompilerParams(vmem_limit_bytes=mib * MIB)


def grid_of(scalars, grid, ins, outs, scratch=()):
    return pltpu.PrefetchScalarGridSpec(
        num_scalar_prefetch=scalars, grid=grid, in_specs=ins, out_specs=outs, scratch_shapes=scratch
    )


def gather_body(parts, after, q_ref, ids_ref, codes_ref, sc_ref, *rest):
    n = len(parts)
    rest = rest[after:]
    outs, token = rest[: 2 * n], rest[2 * n]
    wide, held, stage, sem_in, sem_out = rest[2 * n + 1 :]
    rows, width = held.shape
    nb = width // LANES
    piece = rows // PIECES
    quarter = rows // 4

    def load(i):
        at = pl.ds(i * piece, piece)
        return pltpu.make_async_copy(codes_ref.at[at], held.at[at], sem_in.at[i])

    for i in range(PIECES):
        load(i).start()
    spread = (
        lax.broadcasted_iota(I32, (3 * nb, width), 0) % nb
        == lax.broadcasted_iota(I32, (3 * nb, width), 1) // LANES
    ).astype(F32).astype(BF)
    for i in range(PIECES):
        load(i).wait()
        r0 = i * piece
        s = sc_ref[:, r0 : r0 + piece]
        hi = s.astype(BF)
        left = s - hi.astype(F32)
        mid = left.astype(BF)
        low = (left - mid.astype(F32)).astype(BF)
        three = jnp.concatenate([hi, mid, low], axis=0)
        scale = lax.dot_general(three, spread, (((0,), (0,)), ((), ())), preferred_element_type=F32)
        for b in range(nb):
            cols = slice(b * LANES, (b + 1) * LANES)
            wide[pl.ds(r0 * nb + b, piece, stride=nb), :] = (
                held[r0 : r0 + piece, cols].astype(F32) * scale[:, cols]
            )
    q = q_ref[0]
    token[0] = q
    size = quarter // 2
    for p in range(2 * n):
        src = (q ^ parts[p // 2]) * quarter + p % 2 * size

        def block(t, carry, p=p, src=src):
            o = pl.multiple_of(t * TB, TB)
            for r in range(TB):
                e = ids_ref[src + o + r]
                stage[r * nb : (r + 1) * nb, :] = wide[pl.ds(pl.multiple_of(e * nb, nb), nb), :]
            d = pl.multiple_of(p * size + o, TB)
            for b in range(nb):
                held[pl.ds(d, TB), b * LANES : (b + 1) * LANES] = stage[
                    pl.ds(b, TB, stride=nb), :
                ].astype(BF)
            pltpu.make_async_copy(
                held.at[pl.ds(d, TB)], outs[p].at[pl.ds(o, TB)], sem_out.at[p]
            ).start()
            return carry

        lax.fori_loop(0, size // TB, block, 0)
    for p in range(2 * n):
        pltpu.make_async_copy(held.at[pl.ds(p * size, size)], outs[p], sem_out.at[p]).wait()


def gather(parts, q, ids, codes, scales_t, after=()):
    rows, width = codes.shape
    nb = scales_t.shape[0]
    n = len(parts)
    return pl.pallas_call(
        functools.partial(gather_body, parts, len(after)),
        grid_spec=grid_of(
            2,
            (),
            [ANY, VMEM] + [ANY] * len(after),
            [ANY] * (2 * n) + [SMEM],
            [
                pltpu.VMEM((rows * nb, LANES), F32),
                pltpu.VMEM((rows, width), BF),
                pltpu.VMEM((TB * nb, LANES), F32),
                pltpu.SemaphoreType.DMA((PIECES,)),
                pltpu.SemaphoreType.DMA((2 * n,)),
            ],
        ),
        out_shape=[jax.ShapeDtypeStruct((rows // 8, width), BF)] * (2 * n) + [TOKEN],
        compiler_params=params(54),
        name="gather_features",
    )(q, ids, codes, scales_t, *after)


def pick_body(owners_ref, q_ref, rec_ref, out_ref, token, held, sem):
    token[0] = q_ref[0]
    n, rounds = out_ref.shape[:2]
    for r in range(rounds):
        held[r] = rec_ref[owners_ref[r]]
    copies = [pltpu.make_async_copy(held, out_ref.at[d], sem.at[d]) for d in range(n)]
    for copy in copies:
        copy.start()
    for copy in copies:
        copy.wait()


def pick(owners, q, rec):
    n, h, w = rec.shape
    rounds = owners.shape[0]
    return pl.pallas_call(
        pick_body,
        grid_spec=grid_of(
            2,
            (),
            [VMEM],
            [pl.BlockSpec(memory_space=pltpu.HBM), SMEM],
            [pltpu.VMEM((rounds, h, w), BF), pltpu.SemaphoreType.DMA((n,))],
        ),
        out_shape=[pltpu.HBM((n, rounds, h, w), BF), TOKEN],
        compiler_params=params(8),
        name="pick_pieces",
    )(owners, q, rec)


def tie_body(*refs):
    pass


def tie(q, x, after=()):
    return pl.pallas_call(
        tie_body,
        grid_spec=grid_of(1, (), [ANY] * (1 + len(after)), ANY),
        out_shape=jax.ShapeDtypeStruct(x.shape, x.dtype),
        input_output_aliases={1: 0},
        compiler_params=params(1),
        name="tie",
    )(q, x, *after)


def lay(raw_ref, t_ref):
    n, rounds, h, w = raw_ref.shape
    per = t_ref.shape[0] // rounds
    for r in range(rounds):
        for d in range(n):
            row = r * per + d // CUTS * h
            t_ref[row : row + h, d % CUTS * w : (d % CUTS + 1) * w] = raw_ref[d, r]


def dots(mine_ref, other_ref, tm, to):
    acc = lax.dot_general(mine_ref[...], tm[...], NT, preferred_element_type=F32)
    return acc + lax.dot_general(other_ref[...], to[...], NT, preferred_element_type=F32)


def send_body(q_ref, mine_ref, other_ref, tm_ref, to_ref, *rest):
    out_ref, token, tm, to = rest[-4:]
    token[0] = q_ref[0]

    @pl.when(pl.program_id(0) == 0)
    def _():
        lay(tm_ref, tm)
        lay(to_ref, to)

    out_ref[...] = dots(mine_ref, other_ref, tm, to).astype(BF)


def send_scores(q, mine, other, raw_m, raw_o, pair, per, after=(), block=512):
    count, width = mine.shape
    n, _, h, w = raw_m.shape
    feats = pl.BlockSpec((block, width), lambda i, *_: (i, 0))
    targets = pl.BlockSpec((n, 2, h, w), lambda i, *_: (0, pair, 0, 0))
    return pl.pallas_call(
        send_body,
        grid_spec=grid_of(
            1,
            (count // block,),
            [feats, feats, targets, targets] + [ANY] * len(after),
            [pl.BlockSpec((block, 2 * per), lambda i, *_: (i, 0)), SMEM],
            [pltpu.VMEM((2 * per, width), BF)] * 2,
        ),
        out_shape=[jax.ShapeDtypeStruct((count, 2 * per), BF), TOKEN],
        compiler_params=params(16),
        name="send_scores",
    )(q, mine, other, raw_m, raw_o, *after)


def near_body(scale, q_ref, mine_ref, other_ref, tm_ref, to_ref, *rest):
    out_ref, token, tm, to = rest[-4:]
    token[0] = q_ref[0]

    @pl.when(pl.program_id(0) == 0)
    def _():
        lay(tm_ref, tm)
        lay(to_ref, to)

    out_ref[...] = dots(mine_ref, other_ref, tm, to) * scale


def near_scores(q, scale, mine, other, raw_m, raw_o, per, half, out, block=256):
    rows, width = mine.shape
    total = per * raw_m.shape[1]
    feats = pl.BlockSpec((block, width), lambda i, *_: (i, 0))
    raw = pl.BlockSpec(raw_m.shape, lambda i, *_: (0, 0, 0, 0))
    given = [] if out is None else [out]
    return pl.pallas_call(
        functools.partial(near_body, scale),
        grid_spec=grid_of(
            1,
            (rows // block,),
            [feats, feats, raw, raw] + [ANY] * len(given),
            [pl.BlockSpec((block, total), lambda i, *_: (i + half * (rows // block), 0)), SMEM],
            [pltpu.VMEM((total, width), BF)] * 2,
        ),
        out_shape=[jax.ShapeDtypeStruct((2 * rows, total), F32), TOKEN],
        input_output_aliases={5: 0} if given else {},
        compiler_params=params(32),
        name="near_scores",
    )(q, mine, other, raw_m, raw_o, *given)


def add_body(scale, got_ref, old_ref, out_ref):
    out_ref[...] = old_ref[...] + got_ref[...].astype(F32) * scale


def add_scores(scale, got, out, pair, start, block=512):
    count, cols = got.shape
    cell = pl.BlockSpec((block, cols), lambda i: (i + start // block, pair))
    return pl.pallas_call(
        functools.partial(add_body, scale),
        grid=(count // block,),
        in_specs=[pl.BlockSpec((block, cols), lambda i: (i, 0)), cell],
        out_specs=cell,
        out_shape=jax.ShapeDtypeStruct(out.shape, F32),
        input_output_aliases={1: 0},
        compiler_params=params(16),
        name="add_scores",
    )(got, out)


def per_device(codes, scales, example_ids, targets, owners):
    n_ckpt = lax.axis_size("ckpt")
    n_wide = lax.axis_size("wide")
    q = lax.axis_index("ckpt")
    width = codes.shape[-1]
    codes, scales_t, ids = codes[0, 0], scales[0, 0].T, example_ids[0]
    other_core = [(i, i ^ 1) for i in range(n_ckpt)]
    other_chip = [(i, i ^ 2) for i in range(n_ckpt)]
    per = targets.shape[0]
    quarter = ids.shape[0] // n_ckpt
    scale = 1.0 / n_ckpt
    q1 = q.reshape(1)

    h, w = per * CUTS // n_wide, width // CUTS
    own = lax.dynamic_slice_in_dim(targets, q * width, width, 1)
    pieces = own.reshape(n_wide // CUTS, h, CUTS, w).transpose(0, 2, 1, 3).reshape(n_wide, h, w)
    rec = lax.all_to_all(pieces, "wide", 0, 0, tiled=True)
    picked, tok = pick(owners, q1, rec)
    raw_m = lax.all_to_all(picked, "wide", 0, 0, tiled=True)

    *feats, tok = gather((3, 2), tok, ids, codes, scales_t)
    mine_far = feats[2:]
    other_far = [lax.ppermute(x, "ckpt", other_core) for x in feats[:2]]
    raw_m = tie(tok, raw_m)
    raw_o = lax.ppermute(raw_m, "ckpt", other_core)

    pairs = owners.shape[0] // 2
    steps = [(pair, half) for pair in range(pairs) for half in range(2)]
    got = []
    for i, (pair, half) in enumerate(steps):
        if i == AHEAD:
            *feats, tok = gather((1, 0), tok, ids, codes, scales_t, got[:1])
        after = [got[i - 3]] if i >= AHEAD else []
        part, tok = send_scores(
            tok, mine_far[half], other_far[half], raw_m, raw_o, pair, per, after
        )
        got.append(lax.ppermute(part, "ckpt", other_chip))
        if i == AHEAD:
            other_near = [
                lax.ppermute(tie(tok, x, got[2 + side : 3 + side]), "ckpt", other_core)
                for side, x in enumerate(feats[:2])
            ]
    mine_near = feats[2:]

    out = None
    for half in range(2):
        out, tok = near_scores(
            tok, scale, mine_near[half], other_near[half], raw_m, raw_o, per, half, out
        )
    for (pair, half), part in zip(steps, got, strict=True):
        out = add_scores(scale, part, out, pair, half * (quarter // 2))
    return out[None]


def solution(mesh):
    return jax.shard_map(
        per_device,
        mesh=mesh,
        in_specs=(
            P("ckpt", "wide", None, None),
            P("ckpt", "wide", None, None),
            P("wide", None),
            P("wide", None),
            P(),
        ),
        out_specs=P("wide", "ckpt", None),
        check_vma=False,
    )
```

```python
import functools

import jax
import jax.numpy as jnp
from jax import lax
from jax.experimental import pallas as pl
from jax.experimental.pallas import tpu as pltpu
from jax.sharding import PartitionSpec as P

BF = jnp.bfloat16
F32 = jnp.float32
I32 = jnp.int32
LANES = 128
PIECES = 8
TB = 128
CUTS = 4
AHEAD = 4
MIB = 1024 * 1024
VMEM = pl.BlockSpec(memory_space=pltpu.VMEM)
SMEM = pl.BlockSpec(memory_space=pltpu.SMEM)
ANY = pl.BlockSpec(memory_space=pl.ANY)
NT = (((1,), (1,)), ((), ()))
TOKEN = jax.ShapeDtypeStruct((1,), I32)


def params(mib):
    return pltpu.CompilerParams(vmem_limit_bytes=mib * MIB)


def grid_of(scalars, grid, ins, outs, scratch=()):
    return pltpu.PrefetchScalarGridSpec(
        num_scalar_prefetch=scalars, grid=grid, in_specs=ins, out_specs=outs, scratch_shapes=scratch
    )


def gather_body(parts, after, q_ref, ids_ref, codes_ref, sc_ref, *rest):
    n = len(parts)
    rest = rest[after:]
    outs, token = rest[: 2 * n], rest[2 * n]
    wide, held, stage, sem_in, sem_out = rest[2 * n + 1 :]
    rows, width = held.shape
    nb = width // LANES
    piece = rows // PIECES
    quarter = rows // 4

    def load(i):
        at = pl.ds(i * piece, piece)
        return pltpu.make_async_copy(codes_ref.at[at], held.at[at], sem_in.at[i])

    for i in range(PIECES):
        load(i).start()
    spread = (
        lax.broadcasted_iota(I32, (3 * nb, width), 0) % nb
        == lax.broadcasted_iota(I32, (3 * nb, width), 1) // LANES
    ).astype(F32).astype(BF)
    for i in range(PIECES):
        load(i).wait()
        r0 = i * piece
        s = sc_ref[:, r0 : r0 + piece]
        hi = s.astype(BF)
        left = s - hi.astype(F32)
        mid = left.astype(BF)
        low = (left - mid.astype(F32)).astype(BF)
        three = jnp.concatenate([hi, mid, low], axis=0)
        scale = lax.dot_general(three, spread, (((0,), (0,)), ((), ())), preferred_element_type=F32)
        for b in range(nb):
            cols = slice(b * LANES, (b + 1) * LANES)
            wide[pl.ds(r0 * nb + b, piece, stride=nb), :] = (
                held[r0 : r0 + piece, cols].astype(F32) * scale[:, cols]
            )
    q = q_ref[0]
    token[0] = q
    size = quarter // 2
    for p in range(2 * n):
        src = (q ^ parts[p // 2]) * quarter + p % 2 * size

        def block(t, carry, p=p, src=src):
            o = pl.multiple_of(t * TB, TB)
            for r in range(TB):
                e = ids_ref[src + o + r]
                stage[r * nb : (r + 1) * nb, :] = wide[pl.ds(pl.multiple_of(e * nb, nb), nb), :]
            d = pl.multiple_of(p * size + o, TB)
            for b in range(nb):
                held[pl.ds(d, TB), b * LANES : (b + 1) * LANES] = stage[
                    pl.ds(b, TB, stride=nb), :
                ].astype(BF)
            pltpu.make_async_copy(
                held.at[pl.ds(d, TB)], outs[p].at[pl.ds(o, TB)], sem_out.at[p]
            ).start()
            return carry

        lax.fori_loop(0, size // TB, block, 0)
    for p in range(2 * n):
        pltpu.make_async_copy(held.at[pl.ds(p * size, size)], outs[p], sem_out.at[p]).wait()


def gather(parts, q, ids, codes, scales_t, after=()):
    rows, width = codes.shape
    nb = scales_t.shape[0]
    n = len(parts)
    return pl.pallas_call(
        functools.partial(gather_body, parts, len(after)),
        grid_spec=grid_of(
            2,
            (),
            [ANY, VMEM] + [ANY] * len(after),
            [ANY] * (2 * n) + [SMEM],
            [
                pltpu.VMEM((rows * nb, LANES), F32),
                pltpu.VMEM((rows, width), BF),
                pltpu.VMEM((TB * nb, LANES), F32),
                pltpu.SemaphoreType.DMA((PIECES,)),
                pltpu.SemaphoreType.DMA((2 * n,)),
            ],
        ),
        out_shape=[jax.ShapeDtypeStruct((rows // 8, width), BF)] * (2 * n) + [TOKEN],
        compiler_params=params(54),
        name="gather_features",
    )(q, ids, codes, scales_t, *after)


def pick_body(owners_ref, q_ref, rec_ref, out_ref, token, held, sem):
    token[0] = q_ref[0]
    m, rounds = held.shape[:2]
    n = out_ref.shape[0] // m
    for r in range(rounds):
        piece = rec_ref[owners_ref[r]]
        for i in range(m):
            held[i, r] = piece
    copies = [
        pltpu.make_async_copy(held, out_ref.at[pl.ds(d * m, m)], sem.at[d]) for d in range(n)
    ]
    for copy in copies:
        copy.start()
    for copy in copies:
        copy.wait()


def pick(owners, q, rec):
    n, h, w = rec.shape
    rounds = owners.shape[0]
    return pl.pallas_call(
        pick_body,
        grid_spec=grid_of(
            2,
            (),
            [VMEM],
            [pl.BlockSpec(memory_space=pltpu.HBM), SMEM],
            [pltpu.VMEM((CUTS, rounds, h, w), BF), pltpu.SemaphoreType.DMA((n // CUTS,))],
        ),
        out_shape=[pltpu.HBM((n, rounds, h, w), BF), TOKEN],
        compiler_params=params(8),
        name="pick_pieces",
    )(owners, q, rec)


def tie_body(*refs):
    pass


def tie(q, x, after=()):
    return pl.pallas_call(
        tie_body,
        grid_spec=grid_of(1, (), [ANY] * (1 + len(after)), ANY),
        out_shape=jax.ShapeDtypeStruct(x.shape, x.dtype),
        input_output_aliases={1: 0},
        compiler_params=params(1),
        name="tie",
    )(q, x, *after)


def lay(raw_ref, t_ref):
    n, rounds, h, w = raw_ref.shape
    per = t_ref.shape[0] // rounds
    for r in range(rounds):
        for d in range(n):
            row = r * per + d // CUTS * h
            t_ref[row : row + h, d % CUTS * w : (d % CUTS + 1) * w] = raw_ref[d, r]


def dots(mine_ref, other_ref, tm, to):
    acc = lax.dot_general(mine_ref[...], tm[...], NT, preferred_element_type=F32)
    return acc + lax.dot_general(other_ref[...], to[...], NT, preferred_element_type=F32)


def send_body(q_ref, mine_ref, other_ref, tm_ref, to_ref, *rest):
    out_ref, token, tm, to = rest[-4:]
    token[0] = q_ref[0]

    @pl.when(pl.program_id(0) == 0)
    def _():
        lay(tm_ref, tm)
        lay(to_ref, to)

    out_ref[...] = dots(mine_ref, other_ref, tm, to).astype(BF)


def send_scores(q, mine, other, raw_m, raw_o, pair, per, after=(), block=512):
    count, width = mine.shape
    n, _, h, w = raw_m.shape
    feats = pl.BlockSpec((block, width), lambda i, *_: (i, 0))
    targets = pl.BlockSpec((n, 2, h, w), lambda i, *_: (0, pair, 0, 0))
    return pl.pallas_call(
        send_body,
        grid_spec=grid_of(
            1,
            (count // block,),
            [feats, feats, targets, targets] + [ANY] * len(after),
            [pl.BlockSpec((block, 2 * per), lambda i, *_: (i, 0)), SMEM],
            [pltpu.VMEM((2 * per, width), BF)] * 2,
        ),
        out_shape=[jax.ShapeDtypeStruct((count, 2 * per), BF), TOKEN],
        compiler_params=params(16),
        name="send_scores",
    )(q, mine, other, raw_m, raw_o, *after)


def near_body(scale, parts, q_ref, mine_ref, other_ref, tm_ref, to_ref, *rest):
    out_ref, token, tm, to = rest[-4:]
    token[0] = q_ref[0]

    @pl.when(pl.program_id(0) == 0)
    def _():
        lay(tm_ref, tm)
        lay(to_ref, to)

    acc = dots(mine_ref, other_ref, tm, to)
    cols = 0
    for part in rest[:parts]:
        first, cols = cols, cols + part.shape[1]
        out_ref[:, first:cols] = (acc[:, first:cols] + part[...].astype(F32)) * scale
    out_ref[:, cols:] = acc[:, cols:] * scale


def near_scores(q, scale, mine, other, raw_m, raw_o, per, half, parts, out, block=256):
    rows, width = mine.shape
    total = per * raw_m.shape[1]
    feats = pl.BlockSpec((block, width), lambda i, *_: (i, 0))
    raw = pl.BlockSpec(raw_m.shape, lambda i, *_: (0, 0, 0, 0))
    given = [] if out is None else [out]
    cells = [pl.BlockSpec((block, p.shape[1]), lambda i, *_: (i, 0)) for p in parts]
    return pl.pallas_call(
        functools.partial(near_body, scale, len(parts)),
        grid_spec=grid_of(
            1,
            (rows // block,),
            [feats, feats, raw, raw] + cells + [ANY] * len(given),
            [pl.BlockSpec((block, total), lambda i, *_: (i + half * (rows // block), 0)), SMEM],
            [pltpu.VMEM((total, width), BF)] * 2,
        ),
        out_shape=[jax.ShapeDtypeStruct((2 * rows, total), F32), TOKEN],
        input_output_aliases={5 + len(parts): 0} if given else {},
        compiler_params=params(32),
        name="near_scores",
    )(q, mine, other, raw_m, raw_o, *parts, *given)


def add_body(scale, got_ref, old_ref, out_ref):
    out_ref[...] = old_ref[...] + got_ref[...].astype(F32) * scale


def add_scores(scale, got, out, pair, start, block=512):
    count, cols = got.shape
    cell = pl.BlockSpec((block, cols), lambda i: (i + start // block, pair))
    return pl.pallas_call(
        functools.partial(add_body, scale),
        grid=(count // block,),
        in_specs=[pl.BlockSpec((block, cols), lambda i: (i, 0)), cell],
        out_specs=cell,
        out_shape=jax.ShapeDtypeStruct(out.shape, F32),
        input_output_aliases={1: 0},
        compiler_params=params(16),
        name="add_scores",
    )(got, out)


def per_device(codes, scales, example_ids, targets, owners):
    n_ckpt = lax.axis_size("ckpt")
    n_wide = lax.axis_size("wide")
    q = lax.axis_index("ckpt")
    width = codes.shape[-1]
    codes, scales_t, ids = codes[0, 0], scales[0, 0].T, example_ids[0]
    other_core = [(i, i ^ 1) for i in range(n_ckpt)]
    other_chip = [(i, i ^ 2) for i in range(n_ckpt)]
    per = targets.shape[0]
    quarter = ids.shape[0] // n_ckpt
    scale = 1.0 / n_ckpt
    q1 = q.reshape(1)

    h, w = per * CUTS // n_wide, width // CUTS
    own = lax.dynamic_slice_in_dim(targets, q * width, width, 1)
    pieces = own.reshape(n_wide // CUTS, h, CUTS, w).transpose(0, 2, 1, 3).reshape(n_wide, h, w)
    rec = lax.all_to_all(pieces, "wide", 0, 0, tiled=True)
    picked, tok = pick(owners, q1, rec)
    raw_m = lax.all_to_all(picked, "wide", 0, 0, tiled=True)

    *feats, tok = gather((3, 2), tok, ids, codes, scales_t)
    mine_far, to_far = feats[2:], feats[1]
    other_far = [lax.ppermute(feats[0], "ckpt", other_core)]
    raw_m = tie(tok, raw_m)
    raw_o = lax.ppermute(raw_m, "ckpt", other_core)

    pairs = owners.shape[0] // 2
    steps = [(pair, half) for pair in range(pairs) for half in range(2)]
    got = []
    for i, (pair, half) in enumerate(steps):
        if i == AHEAD:
            *feats, tok = gather((1, 0), tok, ids, codes, scales_t, got[:1])
        after = [got[i - 3]] if i >= AHEAD else []
        part, tok = send_scores(
            tok, mine_far[half], other_far[half], raw_m, raw_o, pair, per, after
        )
        got.append(lax.ppermute(part, "ckpt", other_chip))
        if i == 0:
            other_far.append(lax.ppermute(tie(tok, to_far), "ckpt", other_core))
        if i == AHEAD:
            other_near = [
                lax.ppermute(tie(tok, x, got[2 + side : 3 + side]), "ckpt", other_core)
                for side, x in enumerate(feats[:2])
            ]
    mine_near = feats[2:]

    out = None
    for half in range(2):
        out, tok = near_scores(
            tok, scale, mine_near[half], other_near[half], raw_m, raw_o, per, half, got[half:-2:2], out
        )
    for (pair, half), part in list(zip(steps, got, strict=True))[-2:]:
        out = add_scores(scale, part, out, pair, half * (quarter // 2))
    return out[None]


def solution(mesh):
    return jax.shard_map(
        per_device,
        mesh=mesh,
        in_specs=(
            P("ckpt", "wide", None, None),
            P("ckpt", "wide", None, None),
            P("wide", None),
            P("wide", None),
            P(),
        ),
        out_specs=P("wide", "ckpt", None),
        check_vma=False,
    )
```

```python
import functools

import jax
import jax.numpy as jnp
from jax import lax
from jax.experimental import pallas as pl
from jax.experimental.pallas import tpu as pltpu
from jax.sharding import PartitionSpec as P

BF = jnp.bfloat16
F32 = jnp.float32
I32 = jnp.int32
LANES = 128
PIECES = 8
TB = 128
CUTS = 4
AHEAD = 5
MIB = 1024 * 1024
VMEM = pl.BlockSpec(memory_space=pltpu.VMEM)
SMEM = pl.BlockSpec(memory_space=pltpu.SMEM)
ANY = pl.BlockSpec(memory_space=pl.ANY)
NT = (((1,), (1,)), ((), ()))
TOKEN = jax.ShapeDtypeStruct((1,), I32)


def params(mib):
    return pltpu.CompilerParams(vmem_limit_bytes=mib * MIB)


def grid_of(scalars, grid, ins, outs, scratch=()):
    return pltpu.PrefetchScalarGridSpec(
        num_scalar_prefetch=scalars, grid=grid, in_specs=ins, out_specs=outs, scratch_shapes=scratch
    )


def gather_body(parts, after, q_ref, ids_ref, codes_ref, sc_ref, *rest):
    n = len(parts)
    rest = rest[after:]
    outs, token = rest[: 2 * n], rest[2 * n]
    wide, held, stage, sem_in, sem_out = rest[2 * n + 1 :]
    rows, width = held.shape
    nb = width // LANES
    piece = rows // PIECES
    quarter = rows // 4

    def load(i):
        at = pl.ds(i * piece, piece)
        return pltpu.make_async_copy(codes_ref.at[at], held.at[at], sem_in.at[i])

    for i in range(PIECES):
        load(i).start()
    spread = (
        lax.broadcasted_iota(I32, (3 * nb, width), 0) % nb
        == lax.broadcasted_iota(I32, (3 * nb, width), 1) // LANES
    ).astype(F32).astype(BF)
    for i in range(PIECES):
        load(i).wait()
        r0 = i * piece
        s = sc_ref[:, r0 : r0 + piece]
        hi = s.astype(BF)
        left = s - hi.astype(F32)
        mid = left.astype(BF)
        low = (left - mid.astype(F32)).astype(BF)
        three = jnp.concatenate([hi, mid, low], axis=0)
        scale = lax.dot_general(three, spread, (((0,), (0,)), ((), ())), preferred_element_type=F32)
        for b in range(nb):
            cols = slice(b * LANES, (b + 1) * LANES)
            wide[pl.ds(r0 * nb + b, piece, stride=nb), :] = (
                held[r0 : r0 + piece, cols].astype(F32) * scale[:, cols]
            )
    q = q_ref[0]
    token[0] = q
    size = quarter // 2
    for p in range(2 * n):
        src = (q ^ parts[p // 2]) * quarter + p % 2 * size

        def block(t, carry, p=p, src=src):
            o = pl.multiple_of(t * TB, TB)
            for r in range(TB):
                e = ids_ref[src + o + r]
                stage[r * nb : (r + 1) * nb, :] = wide[pl.ds(pl.multiple_of(e * nb, nb), nb), :]
            d = pl.multiple_of(p * size + o, TB)
            for b in range(nb):
                held[pl.ds(d, TB), b * LANES : (b + 1) * LANES] = stage[
                    pl.ds(b, TB, stride=nb), :
                ].astype(BF)
            pltpu.make_async_copy(
                held.at[pl.ds(d, TB)], outs[p].at[pl.ds(o, TB)], sem_out.at[p]
            ).start()
            return carry

        lax.fori_loop(0, size // TB, block, 0)
    for p in range(2 * n):
        pltpu.make_async_copy(held.at[pl.ds(p * size, size)], outs[p], sem_out.at[p]).wait()


def gather(parts, q, ids, codes, scales_t, after=()):
    rows, width = codes.shape
    nb = scales_t.shape[0]
    n = len(parts)
    return pl.pallas_call(
        functools.partial(gather_body, parts, len(after)),
        grid_spec=grid_of(
            2,
            (),
            [ANY, VMEM] + [ANY] * len(after),
            [ANY] * (2 * n) + [SMEM],
            [
                pltpu.VMEM((rows * nb, LANES), F32),
                pltpu.VMEM((rows, width), BF),
                pltpu.VMEM((TB * nb, LANES), F32),
                pltpu.SemaphoreType.DMA((PIECES,)),
                pltpu.SemaphoreType.DMA((2 * n,)),
            ],
        ),
        out_shape=[jax.ShapeDtypeStruct((rows // 8, width), BF)] * (2 * n) + [TOKEN],
        compiler_params=params(54),
        name="gather_features",
    )(q, ids, codes, scales_t, *after)


def pick_body(owners_ref, q_ref, rec_ref, out_ref, token, held, sem):
    token[0] = q_ref[0]
    m, rounds = held.shape[:2]
    n = out_ref.shape[0] // m
    for r in range(rounds):
        piece = rec_ref[owners_ref[r]]
        for i in range(m):
            held[i, r] = piece
    copies = [
        pltpu.make_async_copy(held, out_ref.at[pl.ds(d * m, m)], sem.at[d]) for d in range(n)
    ]
    for copy in copies:
        copy.start()
    for copy in copies:
        copy.wait()


def pick(owners, q, rec):
    n, h, w = rec.shape
    rounds = owners.shape[0]
    return pl.pallas_call(
        pick_body,
        grid_spec=grid_of(
            2,
            (),
            [VMEM],
            [pl.BlockSpec(memory_space=pltpu.HBM), SMEM],
            [pltpu.VMEM((CUTS, rounds, h, w), BF), pltpu.SemaphoreType.DMA((n // CUTS,))],
        ),
        out_shape=[pltpu.HBM((n, rounds, h, w), BF), TOKEN],
        compiler_params=params(8),
        name="pick_pieces",
    )(owners, q, rec)


def tie_body(*refs):
    pass


def tie(q, x, after=()):
    return pl.pallas_call(
        tie_body,
        grid_spec=grid_of(1, (), [ANY] * (1 + len(after)), ANY),
        out_shape=jax.ShapeDtypeStruct(x.shape, x.dtype),
        input_output_aliases={1: 0},
        compiler_params=params(1),
        name="tie",
    )(q, x, *after)


def lay(raw_ref, t_ref):
    n, rounds, h, w = raw_ref.shape
    per = t_ref.shape[0] // rounds
    for r in range(rounds):
        for d in range(n):
            row = r * per + d // CUTS * h
            t_ref[row : row + h, d % CUTS * w : (d % CUTS + 1) * w] = raw_ref[d, r]


def dots(mine_ref, other_ref, tm, to):
    acc = lax.dot_general(mine_ref[...], tm[...], NT, preferred_element_type=F32)
    return acc + lax.dot_general(other_ref[...], to[...], NT, preferred_element_type=F32)


def send_body(q_ref, mine_ref, other_ref, tm_ref, to_ref, *rest):
    out_ref, token, tm, to = rest[-4:]
    token[0] = q_ref[0]

    @pl.when(pl.program_id(0) == 0)
    def _():
        lay(tm_ref, tm)
        lay(to_ref, to)

    out_ref[...] = dots(mine_ref, other_ref, tm, to).astype(BF)


def send_scores(q, mine, other, raw_m, raw_o, pair, per, start, count, after=(), block=512):
    width = mine.shape[1]
    n, _, h, w = raw_m.shape
    feats = pl.BlockSpec((block, width), lambda i, *_: (i + start // block, 0))
    targets = pl.BlockSpec((n, 2, h, w), lambda i, *_: (0, pair, 0, 0))
    return pl.pallas_call(
        send_body,
        grid_spec=grid_of(
            1,
            (count // block,),
            [feats, feats, targets, targets] + [ANY] * len(after),
            [pl.BlockSpec((block, 2 * per), lambda i, *_: (i, 0)), SMEM],
            [pltpu.VMEM((2 * per, width), BF)] * 2,
        ),
        out_shape=[jax.ShapeDtypeStruct((count, 2 * per), BF), TOKEN],
        compiler_params=params(16),
        name="send_scores",
    )(q, mine, other, raw_m, raw_o, *after)


def near_body(scale, parts, q_ref, mine_ref, other_ref, tm_ref, to_ref, *rest):
    out_ref, token, tm, to = rest[-4:]
    token[0] = q_ref[0]

    @pl.when(pl.program_id(0) == 0)
    def _():
        lay(tm_ref, tm)
        lay(to_ref, to)

    acc = dots(mine_ref, other_ref, tm, to)
    cols = 0
    for part in rest[:parts]:
        first, cols = cols, cols + part.shape[1]
        out_ref[:, first:cols] = (acc[:, first:cols] + part[...].astype(F32)) * scale
    out_ref[:, cols:] = acc[:, cols:] * scale


def near_scores(q, scale, mine, other, raw_m, raw_o, per, half, parts, out, block=256):
    rows, width = mine.shape
    total = per * raw_m.shape[1]
    feats = pl.BlockSpec((block, width), lambda i, *_: (i, 0))
    raw = pl.BlockSpec(raw_m.shape, lambda i, *_: (0, 0, 0, 0))
    given = [] if out is None else [out]
    cells = [pl.BlockSpec((block, p.shape[1]), lambda i, *_: (i, 0)) for p in parts]
    return pl.pallas_call(
        functools.partial(near_body, scale, len(parts)),
        grid_spec=grid_of(
            1,
            (rows // block,),
            [feats, feats, raw, raw] + cells + [ANY] * len(given),
            [pl.BlockSpec((block, total), lambda i, *_: (i + half * (rows // block), 0)), SMEM],
            [pltpu.VMEM((total, width), BF)] * 2,
        ),
        out_shape=[jax.ShapeDtypeStruct((2 * rows, total), F32), TOKEN],
        input_output_aliases={5 + len(parts): 0} if given else {},
        compiler_params=params(32),
        name="near_scores",
    )(q, mine, other, raw_m, raw_o, *parts, *given)


def add_body(scale, got_ref, old_ref, out_ref):
    out_ref[...] = old_ref[...] + got_ref[...].astype(F32) * scale


def add_scores(scale, got, out, pair, start, block=512):
    count, cols = got.shape
    cell = pl.BlockSpec((block, cols), lambda i: (i + start // block, pair))
    return pl.pallas_call(
        functools.partial(add_body, scale),
        grid=(count // block,),
        in_specs=[pl.BlockSpec((block, cols), lambda i: (i, 0)), cell],
        out_specs=cell,
        out_shape=jax.ShapeDtypeStruct(out.shape, F32),
        input_output_aliases={1: 0},
        compiler_params=params(16),
        name="add_scores",
    )(got, out)


def per_device(codes, scales, example_ids, targets, owners):
    n_ckpt = lax.axis_size("ckpt")
    n_wide = lax.axis_size("wide")
    q = lax.axis_index("ckpt")
    width = codes.shape[-1]
    codes, scales_t, ids = codes[0, 0], scales[0, 0].T, example_ids[0]
    other_core = [(i, i ^ 1) for i in range(n_ckpt)]
    other_chip = [(i, i ^ 2) for i in range(n_ckpt)]
    per = targets.shape[0]
    quarter = ids.shape[0] // n_ckpt
    scale = 1.0 / n_ckpt
    q1 = q.reshape(1)

    h, w = per * CUTS // n_wide, width // CUTS
    own = lax.dynamic_slice_in_dim(targets, q * width, width, 1)
    pieces = own.reshape(n_wide // CUTS, h, CUTS, w).transpose(0, 2, 1, 3).reshape(n_wide, h, w)
    rec = lax.all_to_all(pieces, "wide", 0, 0, tiled=True)
    picked, tok = pick(owners, q1, rec)
    raw_m = lax.all_to_all(picked, "wide", 0, 0, tiled=True)

    *feats, tok = gather((3, 2), tok, ids, codes, scales_t)
    mine_far, to_far = feats[2:], feats[1]
    other_far = [lax.ppermute(feats[0], "ckpt", other_core)]
    raw_m = tie(tok, raw_m)
    raw_o = lax.ppermute(raw_m, "ckpt", other_core)

    size = quarter // 2
    head = owners.shape[0] // 2 - 1
    steps = [(head, 0, 0, size // 2), (head, 0, size // 2, size // 2), (head, 1, 0, size)]
    steps += [(pair, half, 0, size) for pair in range(head) for half in range(2)]
    got = []
    for i, (pair, half, start, count) in enumerate(steps):
        if i == AHEAD:
            *feats, tok = gather((1, 0), tok, ids, codes, scales_t, got[:2])
        after = [got[i - 3]] if i >= 3 else []
        part, tok = send_scores(
            tok, mine_far[half], other_far[half], raw_m, raw_o, pair, per, start, count, after
        )
        got.append(lax.ppermute(part, "ckpt", other_chip))
        if i == 0:
            other_far.append(lax.ppermute(tie(tok, to_far), "ckpt", other_core))
        if i == AHEAD:
            other_near = [
                lax.ppermute(tie(tok, x, got[3 + side : 4 + side]), "ckpt", other_core)
                for side, x in enumerate(feats[:2])
            ]
    mine_near = feats[2:]

    out = None
    for half in range(2):
        out, tok = near_scores(
            tok, scale, mine_near[half], other_near[half], raw_m, raw_o, per, half, got[3 + half : 4 + half], out
        )
    for i in (0, 1, 2, *range(AHEAD, len(steps))):
        pair, half, start, _ = steps[i]
        out = add_scores(scale, got[i], out, pair, half * size + start)
    return out[None]


def solution(mesh):
    return jax.shard_map(
        per_device,
        mesh=mesh,
        in_specs=(
            P("ckpt", "wide", None, None),
            P("ckpt", "wide", None, None),
            P("wide", None),
            P("wide", None),
            P(),
        ),
        out_specs=P("wide", "ckpt", None),
        check_vma=False,
    )
```
